32 devices in a mesh: sta: 4 (over z), tm: 8 (over y, x, core).
Axes of the slice: x: 2, y: 2, z: 4, core: 2. Of those that a mesh axis runs over, the one named last changes fastest.
Arguments:
- waveforms: bfloat16 [16, 3, 16384], P('sta', None, 'tm'), may hold values from -90 to 90, as said below
- templates: bfloat16 [16, 768, 256], P('sta'), may hold values from -21 to 21
- moveouts: int32 [16, 256], P('sta'), may hold values from 0 to 1791, as said below
- gap_masks: int32 [16, 8], P('sta'), may hold values 0 or 1
Outputs:
- stack: float32 [256, 16384], P('sta', 'tm')
The draws below stay inside these ranges and needn't reach their ends.
Inputs may be any that keep to these rules, and one draw needn't show every extreme that they name: `waveforms`: each waveform sample lies within -90 to 90. `moveouts`: moveouts are whole sample counts, below 1792.
All inputs are finite; a program needn't handle non-finite values. No bound on the sum of `gap_masks` on one device may be relied on, other than what follows from the above.
Results may differ from the reference program's by a relative error of at most 0.0003.
Values may be sent and summed in bfloat16 or wider, within the bound.
A program may use at most 64 MiB of HBM per device.

```python
import jax
import jax.numpy as jnp
from jax import lax

TLEN = 256
NTEMP = 256
MAXMOVE = 1792
BLOCK = 2048
STATIONS = 16
NBLK = 8
SAMPLES = 16384


def draw_waveforms(key, part):
    first, second, third = jax.random.split(key, 3)
    noise = jnp.clip(jax.random.normal(first, (STATIONS, 3, SAMPLES), jnp.float32), -6.0, 6.0)
    spread = 1.2
    envelope = jnp.exp(jax.random.uniform(second, (STATIONS, 3, SAMPLES // 16), jnp.float32, -spread, spread))
    envelope = jnp.repeat(envelope, 16, axis=2)
    station_gain = jnp.exp(jax.random.uniform(third, (STATIONS, 1, 1), jnp.float32, -1.5, 1.5))
    return (noise * envelope * station_gain).astype(jnp.bfloat16)


def draw_templates(key, part):
    first, second = jax.random.split(key, 2)
    noise = jnp.clip(jax.random.normal(first, (STATIONS, 3 * TLEN, NTEMP), jnp.float32), -6.0, 6.0)
    scales = jnp.exp(jax.random.uniform(second, (STATIONS, 1, NTEMP), jnp.float32, -1.2, 1.2))
    return (noise * scales).astype(jnp.bfloat16)


def draw_moveouts(key, part):
    first, second, third = jax.random.split(key, 3)
    count = STATIONS * NTEMP
    values = jax.random.randint(first, (STATIONS, NTEMP), 0, MAXMOVE, jnp.int32)
    position = jnp.arange(count, dtype=jnp.int32).reshape(STATIONS, NTEMP)
    highest = jax.random.randint(second, (), 0, count, jnp.int32)
    lowest = (highest + 1 + jax.random.randint(third, (), 0, count - 1, jnp.int32)) % count
    values = jnp.where(position == highest, MAXMOVE - 1, values)
    values = jnp.where(position == lowest, 0, values)
    return values.astype(jnp.int32)


def touch_ends(entries, stream_key, low, high):
    longest = entries.shape.index(max(entries.shape))
    spots = []
    for shift in (0, 1):
        where = [jax.random.randint(jax.random.fold_in(stream_key, axis), (), 0, length) for axis, length in enumerate(entries.shape)]
        where[longest] = (where[longest] + shift) % entries.shape[longest]
        spots.append(tuple(where))
    return entries.at[spots[0]].set(low).at[spots[1]].set(high)


def setup_inputs(seed: int = 0) -> dict:
    key_list = jax.random.split(jax.random.key(seed), 5)
    return {
        "waveforms": draw_waveforms(jax.random.fold_in(key_list[4], 71), 0),
        "templates": draw_templates(jax.random.fold_in(key_list[4], 71), 0),
        "moveouts": draw_moveouts(jax.random.fold_in(key_list[4], 71), 0),
        "gap_masks": touch_ends((jax.random.randint(key_list[3], (STATIONS, NBLK), 0, 4) < 3).astype(jnp.int32), jax.random.fold_in(key_list[3], 1), 0, 1),
    }


EPSILON = 1e-06

def hankel(series, row_count):
    length = series.shape[-1]
    repeated = jnp.tile(series, (1,) * (series.ndim - 1) + (TLEN + 1,))
    flattened = repeated[..., :TLEN * (length + 1)]
    return flattened.reshape(series.shape[:-1] + (TLEN, length + 1))[..., :row_count]

def correlate(signal, template_s, row_count):
    hankel_mat = hankel(signal, row_count).reshape(3 * TLEN, row_count)
    product = lax.dot_general(template_s.astype(jnp.float32), hankel_mat.astype(jnp.float32), (((0,), (0,)), ((), ())))
    squares = lax.optimization_barrier(jnp.sum(signal.astype(jnp.float32) ** 2, axis=0))
    energy = lax.optimization_barrier(jnp.sum(hankel(squares, row_count), axis=0)) / (3 * TLEN)
    tmpl_energy = lax.optimization_barrier(jnp.mean(template_s.astype(jnp.float32) ** 2, axis=0))
    scaling = 3 * TLEN * jnp.sqrt((energy + EPSILON)[None, :] * (tmpl_energy + EPSILON)[:, None])
    return product / scaling

def reference(waveforms, templates, moveouts, gap_masks):
    zeros_tail = jnp.zeros((STATIONS, 3, TLEN - 1), jnp.bfloat16)
    extended = jnp.concatenate([waveforms, zeros_tail], axis=2)
    alive_rows = jnp.repeat(gap_masks.astype(jnp.float32), BLOCK, axis=1)

    def station(running, inputs):
        signal, template_s, lag_row, alive_row = inputs
        normalized = correlate(signal, template_s, SAMPLES) * alive_row[None, :]
        padded = jnp.concatenate([normalized, jnp.zeros((NTEMP, MAXMOVE), jnp.float32)], axis=1)
        shifted = jax.vmap(lambda values, lag_val: lax.dynamic_slice_in_dim(values, lag_val, SAMPLES))(padded, lag_row)
        return (running + shifted, None)
    stacked, _ = lax.scan(station, jnp.zeros((NTEMP, SAMPLES), jnp.float32), (extended, templates, moveouts, alive_rows))
    return stacked
```

```python
import functools

import jax
import jax.numpy as jnp
from jax import lax
from jax.experimental import pallas as pl
from jax.experimental.pallas import tpu as pltpu
from jax.sharding import PartitionSpec as P

TLEN = 256
MAXMOVE = 1792
BLOCK = 2048
EPSILON = 1e-06
WIN = 2 * BLOCK
COLS = BLOCK + MAXMOVE
LANES = 128
ROWS = COLS // LANES
OUTR = BLOCK // LANES
TILE = 256


def shifted(block, axis, distance):
    devices = range(lax.axis_size(axis))
    route = [(i - distance, i) for i in devices if i - distance in devices]
    return lax.ppermute(block, axis, route)


def left(value, amount):
    size = value.shape[-1]
    return value if amount % size == 0 else pltpu.roll(value, (-amount) % size, axis=1)


def correlate_kernel(sta_count, ntemp, x_ref, w_ref, lag_ref, gap_ref, out_ref, hank, scale, corr, stack):
    groups = ntemp // 8
    corr_rows = groups * ROWS * 8

    def station(s, carry):
        wave = x_ref[s].astype(jnp.float32)
        run = jnp.sum(wave * wave, axis=0, keepdims=True)
        step = 1
        while step < TLEN:
            run = run + left(run, step)
            step *= 2
        row = lax.rsqrt(run / (3 * TLEN) + EPSILON) * (1.0 / (3 * TLEN))
        lane = lax.broadcasted_iota(jnp.int32, (1, WIN), 1)
        alive = jnp.where(lane < BLOCK, gap_ref[s, 0], gap_ref[s, 1]).astype(jnp.float32)
        scale[...] = jnp.broadcast_to(row * alive, (8, WIN))
        sub = lax.broadcasted_iota(jnp.int32, (16, WIN), 0)
        for c in range(3):
            base = jnp.broadcast_to(wave[c : c + 1], (16, WIN))
            for bit in (1, 2, 4, 8):
                base = jnp.where((sub & bit) != 0, left(base, bit), base)
            for a in range(8):
                hank[c, 16 * a : 16 * (a + 1), :] = left(base, 16 * a).astype(jnp.bfloat16)
        wt = w_ref[s]
        wf = wt.astype(jnp.float32)
        te = jnp.sum(wf * wf, axis=1, keepdims=True) / (3 * TLEN)
        tscale = lax.rsqrt(te + EPSILON)

        def tile(i, carry):
            start = pl.multiple_of(i * TILE, TILE)
            parts = []
            for c in range(3):
                parts.append(hank[c, :, pl.ds(start, TILE)])
                parts.append(hank[c, :, pl.ds(start + LANES, TILE)])
            rhs = jnp.concatenate(parts, axis=0)
            prod = lax.dot_general(wt, rhs, (((1,), (0,)), ((), ())), preferred_element_type=jnp.float32)
            prod = prod * tscale * scale[0:1, pl.ds(start, TILE)]
            for h in range(TILE // LANES):
                for g in range(groups):
                    at = s * corr_rows + g * ROWS * 8 + (i * (TILE // LANES) + h) * 8
                    corr[pl.ds(pl.multiple_of(at, 8), 8), :] = prod[8 * g : 8 * g + 8, LANES * h : LANES * (h + 1)]
            return carry

        lax.fori_loop(0, COLS // TILE, tile, 0)
        return carry

    lax.fori_loop(0, sta_count, station, 0)
    lanes = lax.broadcasted_iota(jnp.int32, (OUTR, LANES), 1)

    def group(g, carry):
        for k in range(8):
            total = None
            for s in range(sta_count):
                lag = lag_ref[s, g * 8 + k]
                p0 = lag // LANES
                r = lag % LANES
                at = s * corr_rows + (g * ROWS + p0) * 8 + k
                lo = corr[pl.ds(at, OUTR, stride=8), :]
                hi = corr[pl.ds(at + 8, OUTR, stride=8), :]
                term = pltpu.roll(jnp.where(lanes >= r, lo, hi), (LANES - r) % LANES, axis=1)
                total = term if total is None else total + term
            stack[pl.ds(k, OUTR, stride=8), :] = total
        for p in range(OUTR):
            out_ref[pl.ds(pl.multiple_of(g * 8, 8), 8), LANES * p : LANES * (p + 1)] = stack[8 * p : 8 * p + 8, :]
        return carry

    lax.fori_loop(0, groups, group, 0)


def correlated(extended, wt, lags, gaps):
    sta_count, ntemp = wt.shape[0], wt.shape[1]
    vmem = pl.BlockSpec(memory_space=pltpu.VMEM)
    smem = pl.BlockSpec(memory_space=pltpu.SMEM)
    return pl.pallas_call(
        functools.partial(correlate_kernel, sta_count, ntemp),
        out_shape=jax.ShapeDtypeStruct((ntemp, BLOCK), jnp.float32),
        in_specs=[vmem, vmem, smem, smem],
        out_specs=vmem,
        scratch_shapes=[
            pltpu.VMEM((3, LANES, WIN), jnp.bfloat16),
            pltpu.VMEM((8, WIN), jnp.float32),
            pltpu.VMEM((sta_count * ntemp * ROWS, LANES), jnp.float32),
            pltpu.VMEM((OUTR * 8, LANES), jnp.float32),
        ],
        compiler_params=pltpu.CompilerParams(vmem_limit_bytes=48 * 1024 * 1024),
        name="correlate",
    )(extended, wt, lags, gaps)


def local(waveforms, templates, moveouts, gap_masks):
    following = shifted(waveforms, "tm", -1)
    extended = jnp.concatenate([waveforms, following], axis=2)
    position = lax.axis_index("tm")
    last = gap_masks.shape[1] - 1
    current = lax.dynamic_slice_in_dim(gap_masks, position, 1, axis=1)
    later = lax.dynamic_slice_in_dim(gap_masks, jnp.minimum(position + 1, last), 1, axis=1)
    gaps = jnp.concatenate([current, later], axis=1)
    wt = jnp.transpose(templates, (0, 2, 1))
    stacked = correlated(extended, wt, moveouts, gaps)
    return lax.psum_scatter(stacked, "sta", scatter_dimension=0, tiled=True)


def solution(mesh):
    in_specs = (P("sta", None, "tm"), P("sta", None, None), P("sta", None), P("sta", None))
    out_specs = P("sta", "tm")
    return jax.shard_map(local, mesh=mesh, in_specs=in_specs, out_specs=out_specs, check_vma=False)
```

```python
import functools

import jax
import jax.numpy as jnp
from jax import lax
from jax.experimental import pallas as pl
from jax.experimental.pallas import tpu as pltpu
from jax.sharding import PartitionSpec as P

TLEN = 256
MAXMOVE = 1792
BLOCK = 2048
EPSILON = 1e-06
WIN = 2 * BLOCK
COLS = BLOCK + MAXMOVE
LANES = 128
ROWS = COLS // LANES + 1
OUTR = BLOCK // LANES
TILE = 1280
LEVELS = 32767.0
MESH = pl.DeviceIdType.MESH


def left(value, amount):
    size = value.shape[-1]
    return value if amount % size == 0 else pltpu.roll(value, (-amount) % size, axis=1)


def stack_kernel(
    peers, blocks, stas, x_ref, w_ref, lag_ref, gap_ref, out_ref,
    nxt, wave, hank, scale, tscale, corr, stack, q_send, m_send, q_recv, m_recv,
    halo_sem, qs_sem, qr_sem, ms_sem, mr_sem,
):
    ntemp = w_ref.shape[1]
    mine = ntemp // peers
    groups = mine // 8
    me_sta = lax.axis_index("sta")
    me_tm = lax.axis_index("tm")
    before = lax.rem(me_tm + blocks - 1, blocks)
    after = lax.rem(me_tm + 1, blocks)
    half = peers // 2

    barrier = pltpu.get_barrier_semaphore()
    for other in (before, after):
        pl.semaphore_signal(barrier, inc=1, device_id={"tm": other}, device_id_type=MESH)
    for d in range(1, peers):
        pl.semaphore_signal(barrier, inc=1, device_id={"sta": lax.rem(me_sta + d, peers)}, device_id_type=MESH)
    pl.semaphore_wait(barrier, peers + 1)

    halo = pltpu.make_async_remote_copy(
        src_ref=x_ref, dst_ref=nxt, send_sem=halo_sem.at[0], recv_sem=halo_sem.at[1],
        device_id={"tm": before}, device_id_type=MESH,
    )
    halo.start()

    def template_scale(s, carry):
        wf = w_ref[s].astype(jnp.float32)
        te = jnp.sum(wf * wf, axis=1, keepdims=True) / (3 * TLEN)
        tscale[pl.ds(pl.multiple_of(s * ntemp, ntemp), ntemp), :] = jnp.broadcast_to(
            lax.rsqrt(te + EPSILON), (ntemp, LANES)
        )
        return carry

    lax.fori_loop(0, stas, template_scale, 0)
    halo.wait()

    present = (me_tm < blocks - 1).astype(jnp.float32)
    wave[:, :BLOCK] = x_ref[...].astype(jnp.float32)
    wave[:, BLOCK:] = nxt[...].astype(jnp.float32) * present
    squares = wave[...] * wave[...]
    run = squares[:stas] + squares[stas : 2 * stas] + squares[2 * stas : 3 * stas]
    step = 1
    while step < TLEN:
        run = run + left(run, step)
        step *= 2
    row = lax.rsqrt(run / (3 * TLEN) + EPSILON) * (1.0 / (3 * TLEN))
    lane = lax.broadcasted_iota(jnp.int32, (stas, WIN), 1)
    sub = lax.broadcasted_iota(jnp.int32, (stas, WIN), 0)
    alive = jnp.zeros((stas, WIN), jnp.int32)
    later = lax.min(me_tm + 1, blocks - 1)
    for s in range(stas):
        alive = jnp.where(sub == s, jnp.where(lane < BLOCK, gap_ref[s, me_tm], gap_ref[s, later]), alive)
    scale[...] = row * alive.astype(jnp.float32)

    sub8 = lax.broadcasted_iota(jnp.int32, (8, WIN), 0)

    def build(i, carry):
        base = jnp.broadcast_to(wave[pl.ds(i, 1), :], (8, WIN))
        for bit in (1, 2, 4):
            base = jnp.where((sub8 & bit) != 0, left(base, bit), base)
        for a in range(8):
            pair = jnp.concatenate([left(base, 16 * a), left(base, 16 * a + 8)], axis=0)
            hank[i, 16 * a : 16 * (a + 1), :] = pair.astype(jnp.bfloat16)
        return carry

    lax.fori_loop(0, 3 * stas, build, 0)

    lanes = lax.broadcasted_iota(jnp.int32, (OUTR, LANES), 1)
    wide = ntemp // 2
    corr_rows = wide * ROWS

    def correlate(side):
        first = pl.multiple_of(side * wide, wide)

        def station(s, carry):
            wt = w_ref[s, pl.ds(first, wide), :]
            ts = tscale[pl.ds(pl.multiple_of(s * ntemp + first, wide), wide), :]

            def tile(i, carry):
                start = pl.multiple_of(i * TILE, TILE)
                parts = []
                for c in range(3):
                    parts.append(hank[c * stas + s, :, pl.ds(start, TILE)])
                    parts.append(hank[c * stas + s, :, pl.ds(start + LANES, TILE)])
                rhs = jnp.concatenate(parts, axis=0)
                prod = lax.dot_general(wt, rhs, (((1,), (0,)), ((), ())), preferred_element_type=jnp.float32)
                prod = prod * scale[pl.ds(s, 1), pl.ds(start, TILE)]
                for h in range(TILE // LANES):
                    part = prod[:, LANES * h : LANES * (h + 1)] * ts
                    for g in range(wide // 8):
                        at = s * corr_rows + g * 8 * ROWS + i * (TILE // LANES) + h
                        corr[pl.ds(at, 8, stride=ROWS), :] = part[8 * g : 8 * g + 8]
                return carry

            return lax.fori_loop(0, COLS // TILE, tile, carry)

        lax.fori_loop(0, stas, station, 0)

    def shift_group(dest, g, slot):
        for k in range(8):
            total = None
            for s in range(stas):
                lag = lag_ref[s, dest * mine + g * 8 + k]
                r = lag & (LANES - 1)
                at = s * corr_rows + (lax.rem(dest, half) * mine + g * 8 + k) * ROWS + (lag >> 7)
                lo = corr[pl.ds(at, OUTR), :]
                hi = corr[pl.ds(at + 1, OUTR), :]
                term = pltpu.roll(jnp.where(lanes >= r, lo, hi), (LANES - r) & (LANES - 1), axis=1)
                total = term if total is None else total + term
            stack[pl.ds(slot * 8 * OUTR + k, OUTR, stride=8), :] = total

    def send_copies(i, dest):
        q_copy = pltpu.make_async_remote_copy(
            src_ref=q_send.at[i], dst_ref=q_recv.at[i], send_sem=qs_sem.at[i], recv_sem=qr_sem.at[i],
            device_id={"sta": dest}, device_id_type=MESH,
        )
        m_copy = pltpu.make_async_remote_copy(
            src_ref=m_send.at[i], dst_ref=m_recv.at[i], send_sem=ms_sem.at[i], recv_sem=mr_sem.at[i],
            device_id={"sta": dest}, device_id_type=MESH,
        )
        return q_copy, m_copy

    def target(i):
        side = me_sta // half
        far = (1 - side) * half + lax.rem(me_sta + i, half)
        near = side * half + lax.rem(me_sta + 1 + i, half)
        return jnp.where(i < half, far, near)

    def chunk(i, carry):
        dest = target(i)

        def pair(gp, carry):
            for h in range(2):
                shift_group(dest, gp * 2 + h, h)
            rows = pl.ds(pl.multiple_of(gp * 16, 16), 16)
            big = None
            vals = []
            for p in range(OUTR):
                v = jnp.concatenate(
                    [stack[8 * p : 8 * p + 8, :], stack[8 * OUTR + 8 * p : 8 * OUTR + 8 * p + 8, :]], axis=0
                )
                vals.append(v)
                big = jnp.abs(v) if big is None else jnp.maximum(big, jnp.abs(v))
            top = jnp.max(big, axis=1, keepdims=True) * 1.01
            top16 = jnp.broadcast_to(jnp.maximum(top, 1e-30), (16, LANES)).astype(jnp.bfloat16)
            m_send[i, rows, :] = top16
            inv = 1.0 / top16.astype(jnp.float32)
            for p in range(OUTR):
                a = jnp.abs(vals[p]) * inv
                root = a * lax.rsqrt(jnp.maximum(a, 1e-30))
                level = (root * LEVELS + 0.5).astype(jnp.int32)
                level = jnp.where(vals[p] < 0.0, -level, level)
                q_send[i, rows, LANES * p : LANES * (p + 1)] = level.astype(jnp.int16)
            return carry

        lax.fori_loop(0, groups // 2, pair, 0)
        for copy in send_copies(i, dest):
            copy.start()
        return carry

    correlate(1 - me_sta // half)
    lax.fori_loop(0, half, chunk, 0)
    correlate(me_sta // half)
    lax.fori_loop(half, peers - 1, chunk, 0)

    def own(g, carry):
        shift_group(me_sta, g, 0)
        for p in range(OUTR):
            out_ref[pl.ds(pl.multiple_of(g * 8, 8), 8), LANES * p : LANES * (p + 1)] = stack[8 * p : 8 * p + 8, :]
        return carry

    lax.fori_loop(0, groups, own, 0)

    def collect(i, carry):
        for copy in send_copies(i, target(i)):
            copy.wait()

        def add(gp, carry):
            rows = pl.ds(pl.multiple_of(gp * 16, 16), 16)
            unit = m_recv[i, rows, :].astype(jnp.float32) * (1.0 / (LEVELS * LEVELS))
            for p in range(OUTR):
                level = q_recv[i, rows, LANES * p : LANES * (p + 1)].astype(jnp.int32).astype(jnp.float32)
                out_ref[rows, LANES * p : LANES * (p + 1)] += level * jnp.abs(level) * unit
            return carry

        return lax.fori_loop(0, mine // 16, add, carry)

    lax.fori_loop(0, peers - 1, collect, 0)


def local(waveforms, templates, moveouts, gap_masks):
    stas, _, block = waveforms.shape
    ntemp = templates.shape[2]
    peers, blocks = lax.axis_size("sta"), lax.axis_size("tm")
    mine = ntemp // peers
    lines = -(-3 * stas // 16) * 16
    x = jnp.transpose(waveforms, (1, 0, 2)).reshape(3 * stas, block)
    x = jnp.pad(x, ((0, lines - 3 * stas), (0, 0)))
    wt = jnp.transpose(templates, (0, 2, 1))
    vmem = pl.BlockSpec(memory_space=pltpu.VMEM)
    smem = pl.BlockSpec(memory_space=pltpu.SMEM)
    dma = pltpu.SemaphoreType.DMA((peers - 1,))
    return pl.pallas_call(
        functools.partial(stack_kernel, peers, blocks, stas),
        out_shape=jax.ShapeDtypeStruct((mine, BLOCK), jnp.float32),
        in_specs=[vmem, vmem, smem, smem],
        out_specs=vmem,
        scratch_shapes=[
            pltpu.VMEM((lines, BLOCK), jnp.bfloat16),
            pltpu.VMEM((lines, WIN), jnp.float32),
            pltpu.VMEM((3 * stas, LANES, WIN), jnp.bfloat16),
            pltpu.VMEM((stas, WIN), jnp.float32),
            pltpu.VMEM((stas * ntemp, LANES), jnp.float32),
            pltpu.VMEM((stas * (ntemp // 2) * ROWS, LANES), jnp.float32),
            pltpu.VMEM((2 * OUTR * 8, LANES), jnp.float32),
            pltpu.VMEM((peers - 1, mine, BLOCK), jnp.int16),
            pltpu.VMEM((peers - 1, mine, LANES), jnp.bfloat16),
            pltpu.VMEM((peers - 1, mine, BLOCK), jnp.int16),
            pltpu.VMEM((peers - 1, mine, LANES), jnp.bfloat16),
            pltpu.SemaphoreType.DMA((2,)),
            dma, dma, dma, dma,
        ],
        compiler_params=pltpu.CompilerParams(
            collective_id=0, has_side_effects=True, vmem_limit_bytes=48 * 1024 * 1024
        ),
        name="stack",
    )(x, wt, moveouts, gap_masks)


def solution(mesh):
    in_specs = (P("sta", None, "tm"), P("sta", None, None), P("sta", None), P("sta", None))
    out_specs = P("sta", "tm")
    return jax.shard_map(local, mesh=mesh, in_specs=in_specs, out_specs=out_specs, check_vma=False)
```

```python
import functools

import jax
import jax.numpy as jnp
from jax import lax
from jax.experimental import pallas as pl
from jax.experimental.pallas import tpu as pltpu
from jax.sharding import PartitionSpec as P

TLEN = 256
MAXMOVE = 1792
BLOCK = 2048
EPSILON = 1e-06
WIN = 2 * BLOCK
COLS = BLOCK + MAXMOVE
LANES = 128
ROWS = COLS // LANES + 1
OUTR = BLOCK // LANES
TILE = 1280
LEVELS = 32767.0
MESH = pl.DeviceIdType.MESH


def left(value, amount):
    size = value.shape[-1]
    return value if amount % size == 0 else pltpu.roll(value, (-amount) % size, axis=1)


def stack_kernel(
    peers, blocks, stas, x_ref, w_ref, lag_ref, gap_ref, out_ref,
    x_mine, nxt, wt_all, wave, hank, scale, tscale, corr, stack, q_send, m_send, q_recv, m_recv,
    halo_sem, qs_sem, qr_sem, ms_sem, mr_sem,
):
    ntemp = w_ref.shape[2]
    mine = ntemp // peers
    groups = mine // 8
    me_sta = lax.axis_index("sta")
    me_tm = lax.axis_index("tm")
    before = lax.rem(me_tm + blocks - 1, blocks)
    after = lax.rem(me_tm + 1, blocks)
    half = peers // 2

    barrier = pltpu.get_barrier_semaphore()
    for other in (before, after):
        pl.semaphore_signal(barrier, inc=1, device_id={"tm": other}, device_id_type=MESH)
    for d in range(1, peers):
        pl.semaphore_signal(barrier, inc=1, device_id={"sta": lax.rem(me_sta + d, peers)}, device_id_type=MESH)
    lines = x_mine.shape[0]
    records = [x_ref[s] for s in range(stas)] + [jnp.zeros((lines - 3 * stas, BLOCK), jnp.bfloat16)]
    wave[:, :BLOCK] = jnp.concatenate([part.astype(jnp.float32) for part in records], axis=0)
    x_mine[...] = wave[:, :BLOCK].astype(jnp.bfloat16)
    pl.semaphore_wait(barrier, peers + 1)

    halo = pltpu.make_async_remote_copy(
        src_ref=x_mine, dst_ref=nxt, send_sem=halo_sem.at[0], recv_sem=halo_sem.at[1],
        device_id={"tm": before}, device_id_type=MESH,
    )
    halo.start()

    def template_scale(s, carry):
        wf = w_ref[s].astype(jnp.float32)
        te = jnp.sum(wf * wf, axis=0, keepdims=True) / (3 * TLEN)
        across = jnp.broadcast_to(lax.rsqrt(te + EPSILON), (LANES, ntemp))
        tscale[pl.ds(pl.multiple_of(s * ntemp, ntemp), ntemp), :] = jnp.transpose(across)
        wt_all[s] = jnp.transpose(w_ref[s])
        return carry

    lax.fori_loop(0, stas, template_scale, 0)

    def build(start, size, keep):
        sub8 = lax.broadcasted_iota(jnp.int32, (8, size), 0)

        def line(i, carry):
            base = jnp.broadcast_to(wave[pl.ds(i, 1), start : start + size], (8, size))
            for bit in (1, 2, 4):
                base = jnp.where((sub8 & bit) != 0, left(base, bit), base)
            for a in range(8):
                pair = jnp.concatenate([left(base, 16 * a), left(base, 16 * a + 8)], axis=0)
                hank[i, 16 * a : 16 * (a + 1), start : start + keep] = pair[:, :keep].astype(jnp.bfloat16)
            return carry

        lax.fori_loop(0, 3 * stas, line, 0)

    build(0, BLOCK, BLOCK - LANES)
    halo.wait()

    present = (me_tm < blocks - 1).astype(jnp.float32)
    wave[:, BLOCK:] = nxt[...].astype(jnp.float32) * present
    squares = wave[...] * wave[...]
    run = jnp.concatenate(
        [squares[3 * s : 3 * s + 1] + squares[3 * s + 1 : 3 * s + 2] + squares[3 * s + 2 : 3 * s + 3] for s in range(stas)],
        axis=0,
    )
    step = 1
    while step < TLEN:
        run = run + left(run, step)
        step *= 2
    row = lax.rsqrt(run / (3 * TLEN) + EPSILON) * (1.0 / (3 * TLEN))
    lane = lax.broadcasted_iota(jnp.int32, (stas, WIN), 1)
    sub = lax.broadcasted_iota(jnp.int32, (stas, WIN), 0)
    alive = jnp.zeros((stas, WIN), jnp.int32)
    later = lax.min(me_tm + 1, blocks - 1)
    for s in range(stas):
        alive = jnp.where(sub == s, jnp.where(lane < BLOCK, gap_ref[s, me_tm], gap_ref[s, later]), alive)
    scale[...] = row * alive.astype(jnp.float32)
    build(BLOCK - LANES, BLOCK + LANES, BLOCK + LANES)

    lanes = lax.broadcasted_iota(jnp.int32, (OUTR, LANES), 1)
    wide = ntemp // 2
    corr_rows = wide * ROWS

    def correlate(side):
        first = pl.multiple_of(side * wide, wide)

        def station(s, carry):
            wt = wt_all[s, pl.ds(first, wide), :]
            ts = tscale[pl.ds(pl.multiple_of(s * ntemp + first, wide), wide), :]

            def tile(i, carry):
                start = pl.multiple_of(i * TILE, TILE)
                parts = []
                for c in range(3):
                    parts.append(hank[3 * s + c, :, pl.ds(start, TILE)])
                    parts.append(hank[3 * s + c, :, pl.ds(start + LANES, TILE)])
                rhs = jnp.concatenate(parts, axis=0)
                prod = lax.dot_general(wt, rhs, (((1,), (0,)), ((), ())), preferred_element_type=jnp.float32)
                prod = prod * scale[pl.ds(s, 1), pl.ds(start, TILE)]
                for h in range(TILE // LANES):
                    part = prod[:, LANES * h : LANES * (h + 1)] * ts
                    for g in range(wide // 8):
                        at = s * corr_rows + g * 8 * ROWS + i * (TILE // LANES) + h
                        corr[pl.ds(at, 8, stride=ROWS), :] = part[8 * g : 8 * g + 8]
                return carry

            return lax.fori_loop(0, COLS // TILE, tile, carry)

        lax.fori_loop(0, stas, station, 0)

    def shift_group(dest, g, slot):
        for k in range(8):
            total = None
            for s in range(stas):
                lag = lag_ref[s, dest * mine + g * 8 + k]
                r = lag & (LANES - 1)
                at = s * corr_rows + (lax.rem(dest, half) * mine + g * 8 + k) * ROWS + (lag >> 7)
                lo = corr[pl.ds(at, OUTR), :]
                hi = corr[pl.ds(at + 1, OUTR), :]
                term = pltpu.roll(jnp.where(lanes >= r, lo, hi), (LANES - r) & (LANES - 1), axis=1)
                total = term if total is None else total + term
            stack[pl.ds(slot * 8 * OUTR + k, OUTR, stride=8), :] = total

    def send_copies(i, dest):
        q_copy = pltpu.make_async_remote_copy(
            src_ref=q_send.at[i], dst_ref=q_recv.at[i], send_sem=qs_sem.at[i], recv_sem=qr_sem.at[i],
            device_id={"sta": dest}, device_id_type=MESH,
        )
        m_copy = pltpu.make_async_remote_copy(
            src_ref=m_send.at[i], dst_ref=m_recv.at[i], send_sem=ms_sem.at[i], recv_sem=mr_sem.at[i],
            device_id={"sta": dest}, device_id_type=MESH,
        )
        return q_copy, m_copy

    def target(i):
        side = me_sta // half
        far = (1 - side) * half + lax.rem(me_sta + i, half)
        near = side * half + lax.rem(me_sta + 1 + i, half)
        return jnp.where(i < half, far, near)

    def chunk(i, carry):
        dest = target(i)

        lane16 = lax.broadcasted_iota(jnp.int32, (16, LANES), 1)

        def pair(gp, tops):
            for h in range(2):
                shift_group(dest, gp * 2 + h, h)
            rows = pl.ds(pl.multiple_of(gp * 16, 16), 16)
            big = None
            vals = []
            for p in range(OUTR):
                v = jnp.concatenate(
                    [stack[8 * p : 8 * p + 8, :], stack[8 * OUTR + 8 * p : 8 * OUTR + 8 * p + 8, :]], axis=0
                )
                vals.append(v)
                big = jnp.abs(v) if big is None else jnp.maximum(big, jnp.abs(v))
            top = jnp.max(big, axis=1, keepdims=True) * 1.01
            top16 = jnp.broadcast_to(jnp.maximum(top, 1e-30), (16, LANES)).astype(jnp.bfloat16)
            top32 = top16.astype(jnp.float32)
            inv = 1.0 / top32
            for p in range(OUTR):
                a = jnp.abs(vals[p]) * inv
                root = a * lax.rsqrt(jnp.maximum(a, 1e-30))
                level = (root * LEVELS + 0.5).astype(jnp.int32)
                level = jnp.where(vals[p] < 0.0, -level, level)
                q_send[i, rows, LANES * p : LANES * (p + 1)] = level.astype(jnp.int16)
            return jnp.where(lane16 == gp, top32, tops)

        tops = lax.fori_loop(0, groups // 2, pair, jnp.zeros((16, LANES), jnp.float32))
        m_send[i] = tops.astype(jnp.bfloat16)
        for copy in send_copies(i, dest):
            copy.start()
        return carry

    correlate(1 - me_sta // half)
    lax.fori_loop(0, half, chunk, 0)
    correlate(me_sta // half)
    lax.fori_loop(half, peers - 1, chunk, 0)

    def own(g, carry):
        shift_group(me_sta, g, 0)
        for p in range(OUTR):
            out_ref[pl.ds(pl.multiple_of(g * 8, 8), 8), LANES * p : LANES * (p + 1)] = stack[8 * p : 8 * p + 8, :]
        return carry

    lax.fori_loop(0, groups, own, 0)

    def collect(i, carry):
        for copy in send_copies(i, target(i)):
            copy.wait()

        def add(gp, carry):
            rows = pl.ds(pl.multiple_of(gp * 16, 16), 16)
            lane16 = lax.broadcasted_iota(jnp.int32, (16, LANES), 1)
            tops = jnp.where(lane16 == gp, m_recv[i].astype(jnp.float32), 0.0)
            unit = jnp.sum(tops, axis=1, keepdims=True) * (1.0 / (LEVELS * LEVELS))
            for p in range(OUTR):
                level = q_recv[i, rows, LANES * p : LANES * (p + 1)].astype(jnp.int32).astype(jnp.float32)
                out_ref[rows, LANES * p : LANES * (p + 1)] += level * jnp.abs(level) * unit
            return carry

        return lax.fori_loop(0, mine // 16, add, carry)

    lax.fori_loop(0, peers - 1, collect, 0)


def local(waveforms, templates, moveouts, gap_masks):
    stas = waveforms.shape[0]
    ntemp = templates.shape[2]
    peers, blocks = lax.axis_size("sta"), lax.axis_size("tm")
    mine = ntemp // peers
    lines = -(-3 * stas // 16) * 16
    vmem = pl.BlockSpec(memory_space=pltpu.VMEM)
    smem = pl.BlockSpec(memory_space=pltpu.SMEM)
    dma = pltpu.SemaphoreType.DMA((peers - 1,))
    return pl.pallas_call(
        functools.partial(stack_kernel, peers, blocks, stas),
        out_shape=jax.ShapeDtypeStruct((mine, BLOCK), jnp.float32),
        in_specs=[vmem, vmem, smem, smem],
        out_specs=vmem,
        scratch_shapes=[
            pltpu.VMEM((lines, BLOCK), jnp.bfloat16),
            pltpu.VMEM((lines, BLOCK), jnp.bfloat16),
            pltpu.VMEM((stas, ntemp, 3 * TLEN), jnp.bfloat16),
            pltpu.VMEM((lines, WIN), jnp.float32),
            pltpu.VMEM((3 * stas, LANES, WIN), jnp.bfloat16),
            pltpu.VMEM((stas, WIN), jnp.float32),
            pltpu.VMEM((stas * ntemp, LANES), jnp.float32),
            pltpu.VMEM((stas * (ntemp // 2) * ROWS, LANES), jnp.float32),
            pltpu.VMEM((2 * OUTR * 8, LANES), jnp.float32),
            pltpu.VMEM((peers - 1, mine, BLOCK), jnp.int16),
            pltpu.VMEM((peers - 1, 16, LANES), jnp.bfloat16),
            pltpu.VMEM((peers - 1, mine, BLOCK), jnp.int16),
            pltpu.VMEM((peers - 1, 16, LANES), jnp.bfloat16),
            pltpu.SemaphoreType.DMA((2,)),
            dma, dma, dma, dma,
        ],
        compiler_params=pltpu.CompilerParams(
            collective_id=0, has_side_effects=True, vmem_limit_bytes=48 * 1024 * 1024
        ),
        name="stack",
    )(waveforms, templates, moveouts, gap_masks)


def solution(mesh):
    in_specs = (P("sta", None, "tm"), P("sta", None, None), P("sta", None), P("sta", None))
    out_specs = P("sta", "tm")
    return jax.shard_map(local, mesh=mesh, in_specs=in_specs, out_specs=out_specs, check_vma=False)
```

```python
import functools

import jax
import jax.numpy as jnp
from jax import lax
from jax.experimental import pallas as pl
from jax.experimental.pallas import tpu as pltpu
from jax.sharding import PartitionSpec as P

TLEN = 256
MAXMOVE = 1792
BLOCK = 2048
EPSILON = 1e-06
WIN = 2 * BLOCK
COLS = BLOCK + MAXMOVE
LANES = 128
ROWS = COLS // LANES + 1
OUTR = BLOCK // LANES
TILE = 1280
LEVELS = 32767.0
MESH = pl.DeviceIdType.MESH


def left(value, amount):
    size = value.shape[-1]
    return value if amount % size == 0 else pltpu.roll(value, (-amount) % size, axis=1)


def stack_kernel(
    peers, blocks, stas, x_ref, w_hbm, lag_hbm, gap_hbm, out_ref,
    w_ref, lag_ref, gap_ref, x_mine, nxt, wt_all, wave, hank, scale, tscale, corr, stack, q_send, m_send, q_recv, m_recv,
    load_sem, halo_sem, qs_sem, qr_sem, ms_sem, mr_sem,
):
    ntemp = w_ref.shape[2]
    mine = ntemp // peers
    groups = mine // 8
    me_sta = lax.axis_index("sta")
    me_tm = lax.axis_index("tm")
    before = lax.rem(me_tm + blocks - 1, blocks)
    after = lax.rem(me_tm + 1, blocks)
    half = peers // 2

    loads = [
        pltpu.make_async_copy(w_hbm, w_ref, load_sem.at[0]),
        pltpu.make_async_copy(lag_hbm, lag_ref, load_sem.at[1]),
        pltpu.make_async_copy(gap_hbm, gap_ref, load_sem.at[2]),
    ]
    for load in loads:
        load.start()
    barrier = pltpu.get_barrier_semaphore()
    for other in (before, after):
        pl.semaphore_signal(barrier, inc=1, device_id={"tm": other}, device_id_type=MESH)
    for d in range(1, peers):
        pl.semaphore_signal(barrier, inc=1, device_id={"sta": lax.rem(me_sta + d, peers)}, device_id_type=MESH)
    lines = x_mine.shape[0]
    records = [x_ref[c] for c in range(3)] + [jnp.zeros((lines - 3 * stas, BLOCK), jnp.bfloat16)]
    wave[:, :BLOCK] = jnp.concatenate([part.astype(jnp.float32) for part in records], axis=0)
    x_mine[...] = wave[:, :BLOCK].astype(jnp.bfloat16)
    pl.semaphore_wait(barrier, peers + 1)

    halo = pltpu.make_async_remote_copy(
        src_ref=x_mine, dst_ref=nxt, send_sem=halo_sem.at[0], recv_sem=halo_sem.at[1],
        device_id={"tm": before}, device_id_type=MESH,
    )
    halo.start()

    wide = ntemp // 2

    def prepare(side):
        first = pl.multiple_of(side * wide, wide)

        def template_scale(s, carry):
            w = w_ref[s, :, pl.ds(first, wide)]
            wf = w.astype(jnp.float32)
            te = jnp.sum(wf * wf, axis=0, keepdims=True) / (3 * TLEN)
            across = jnp.broadcast_to(lax.rsqrt(te + EPSILON), (LANES, wide))
            tscale[pl.ds(pl.multiple_of(s * wide, wide), wide), :] = jnp.transpose(across)
            wt_all[s] = jnp.transpose(w)
            return carry

        lax.fori_loop(0, stas, template_scale, 0)

    def build(start, size, keep):
        sub8 = lax.broadcasted_iota(jnp.int32, (8, size), 0)

        def line(i, carry):
            base = jnp.broadcast_to(wave[pl.ds(i, 1), start : start + size], (8, size))
            for bit in (1, 2, 4):
                base = jnp.where((sub8 & bit) != 0, left(base, bit), base)
            for a in range(8):
                pair = jnp.concatenate([left(base, 16 * a), left(base, 16 * a + 8)], axis=0)
                hank[i, 16 * a : 16 * (a + 1), start : start + keep] = pair[:, :keep].astype(jnp.bfloat16)
            return carry

        lax.fori_loop(0, 3 * stas, line, 0)

    build(0, BLOCK, BLOCK - LANES)
    for load in loads:
        load.wait()
    prepare(1 - me_sta // half)
    halo.wait()

    present = (me_tm < blocks - 1).astype(jnp.float32)
    wave[:, BLOCK:] = nxt[...].astype(jnp.float32) * present
    squares = wave[...] * wave[...]
    run = squares[:stas] + squares[stas : 2 * stas] + squares[2 * stas : 3 * stas]
    step = 1
    while step < TLEN:
        run = run + left(run, step)
        step *= 2
    row = lax.rsqrt(run / (3 * TLEN) + EPSILON) * (1.0 / (3 * TLEN))
    lane = lax.broadcasted_iota(jnp.int32, (stas, WIN), 1)
    sub = lax.broadcasted_iota(jnp.int32, (stas, WIN), 0)
    alive = jnp.zeros((stas, WIN), jnp.int32)
    later = lax.min(me_tm + 1, blocks - 1)
    for s in range(stas):
        alive = jnp.where(sub == s, jnp.where(lane < BLOCK, gap_ref[s, me_tm], gap_ref[s, later]), alive)
    scale[...] = row * alive.astype(jnp.float32)
    build(BLOCK - LANES, BLOCK + LANES, BLOCK + LANES)

    lanes = lax.broadcasted_iota(jnp.int32, (OUTR, LANES), 1)
    corr_rows = wide * ROWS

    def correlate():
        def station(s, carry):
            wt = wt_all[s]
            ts = tscale[pl.ds(pl.multiple_of(s * wide, wide), wide), :]

            def tile(i, carry):
                start = pl.multiple_of(i * TILE, TILE)
                parts = []
                for c in range(3):
                    parts.append(hank[c * stas + s, :, pl.ds(start, TILE)])
                    parts.append(hank[c * stas + s, :, pl.ds(start + LANES, TILE)])
                rhs = jnp.concatenate(parts, axis=0)
                prod = lax.dot_general(wt, rhs, (((1,), (0,)), ((), ())), preferred_element_type=jnp.float32)
                prod = prod * scale[pl.ds(s, 1), pl.ds(start, TILE)]
                for h in range(TILE // LANES):
                    part = prod[:, LANES * h : LANES * (h + 1)] * ts
                    for g in range(wide // 8):
                        at = s * corr_rows + g * 8 * ROWS + i * (TILE // LANES) + h
                        corr[pl.ds(at, 8, stride=ROWS), :] = part[8 * g : 8 * g + 8]
                return carry

            return lax.fori_loop(0, COLS // TILE, tile, carry)

        lax.fori_loop(0, stas, station, 0)

    def shift_group(dest, g, slot):
        for k in range(8):
            total = None
            for s in range(stas):
                lag = lag_ref[s, dest * mine + g * 8 + k]
                r = lag & (LANES - 1)
                at = s * corr_rows + (lax.rem(dest, half) * mine + g * 8 + k) * ROWS + (lag >> 7)
                lo = corr[pl.ds(at, OUTR), :]
                hi = corr[pl.ds(at + 1, OUTR), :]
                term = pltpu.roll(jnp.where(lanes >= r, lo, hi), (LANES - r) & (LANES - 1), axis=1)
                total = term if total is None else total + term
            stack[pl.ds(slot * 8 * OUTR + k, OUTR, stride=8), :] = total

    def send_copies(i, dest):
        q_copy = pltpu.make_async_remote_copy(
            src_ref=q_send.at[i], dst_ref=q_recv.at[i], send_sem=qs_sem.at[i], recv_sem=qr_sem.at[i],
            device_id={"sta": dest}, device_id_type=MESH,
        )
        m_copy = pltpu.make_async_remote_copy(
            src_ref=m_send.at[i], dst_ref=m_recv.at[i], send_sem=ms_sem.at[i], recv_sem=mr_sem.at[i],
            device_id={"sta": dest}, device_id_type=MESH,
        )
        return q_copy, m_copy

    def target(i):
        side = me_sta // half
        far = (1 - side) * half + lax.rem(me_sta + i, half)
        near = side * half + lax.rem(me_sta + 1 + i, half)
        return jnp.where(i < half, far, near)

    def chunk(i, carry):
        dest = target(i)

        lane16 = lax.broadcasted_iota(jnp.int32, (16, LANES), 1)

        def pair(gp, tops):
            for h in range(2):
                shift_group(dest, gp * 2 + h, h)
            rows = pl.ds(pl.multiple_of(gp * 16, 16), 16)
            big = None
            vals = []
            for p in range(OUTR):
                v = jnp.concatenate(
                    [stack[8 * p : 8 * p + 8, :], stack[8 * OUTR + 8 * p : 8 * OUTR + 8 * p + 8, :]], axis=0
                )
                vals.append(v)
                big = jnp.abs(v) if big is None else jnp.maximum(big, jnp.abs(v))
            top = jnp.max(big, axis=1, keepdims=True) * 1.01
            top16 = jnp.broadcast_to(jnp.maximum(top, 1e-30), (16, LANES)).astype(jnp.bfloat16)
            top32 = top16.astype(jnp.float32)
            inv = 1.0 / top32
            for p in range(OUTR):
                a = jnp.abs(vals[p]) * inv
                root = a * lax.rsqrt(jnp.maximum(a, 1e-30))
                level = (root * LEVELS + 0.5).astype(jnp.int32)
                level = jnp.where(vals[p] < 0.0, -level, level)
                q_send[i, rows, LANES * p : LANES * (p + 1)] = level.astype(jnp.int16)
            return jnp.where(lane16 == gp, top32, tops)

        tops = lax.fori_loop(0, groups // 2, pair, jnp.zeros((16, LANES), jnp.float32))
        m_send[i] = tops.astype(jnp.bfloat16)
        for copy in send_copies(i, dest):
            copy.start()
        return carry

    correlate()
    lax.fori_loop(0, half, chunk, 0)
    prepare(me_sta // half)
    correlate()
    lax.fori_loop(half, peers - 1, chunk, 0)

    def own(g, carry):
        shift_group(me_sta, g, 0)
        for p in range(OUTR):
            out_ref[pl.ds(pl.multiple_of(g * 8, 8), 8), LANES * p : LANES * (p + 1)] = stack[8 * p : 8 * p + 8, :]
        return carry

    lax.fori_loop(0, groups, own, 0)

    def collect(i, carry):
        for copy in send_copies(i, target(i)):
            copy.wait()

        def add(gp, carry):
            rows = pl.ds(pl.multiple_of(gp * 16, 16), 16)
            lane16 = lax.broadcasted_iota(jnp.int32, (16, LANES), 1)
            tops = jnp.where(lane16 == gp, m_recv[i].astype(jnp.float32), 0.0)
            unit = jnp.sum(tops, axis=1, keepdims=True) * (1.0 / (LEVELS * LEVELS))
            for p in range(OUTR):
                level = q_recv[i, rows, LANES * p : LANES * (p + 1)].astype(jnp.int32).astype(jnp.float32)
                out_ref[rows, LANES * p : LANES * (p + 1)] += level * jnp.abs(level) * unit
            return carry

        return lax.fori_loop(0, mine // 16, add, carry)

    lax.fori_loop(0, peers - 1, collect, 0)


def local(waveforms, templates, moveouts, gap_masks):
    stas = waveforms.shape[0]
    ntemp = templates.shape[2]
    peers, blocks = lax.axis_size("sta"), lax.axis_size("tm")
    mine = ntemp // peers
    lines = -(-3 * stas // 16) * 16
    vmem = pl.BlockSpec(memory_space=pltpu.VMEM)
    hbm = pl.BlockSpec(memory_space=pltpu.HBM)
    dma = pltpu.SemaphoreType.DMA((peers - 1,))
    return pl.pallas_call(
        functools.partial(stack_kernel, peers, blocks, stas),
        out_shape=jax.ShapeDtypeStruct((mine, BLOCK), jnp.float32),
        in_specs=[vmem, hbm, hbm, hbm],
        out_specs=vmem,
        scratch_shapes=[
            pltpu.VMEM(templates.shape, jnp.bfloat16),
            pltpu.SMEM(moveouts.shape, jnp.int32),
            pltpu.SMEM(gap_masks.shape, jnp.int32),
            pltpu.VMEM((lines, BLOCK), jnp.bfloat16),
            pltpu.VMEM((lines, BLOCK), jnp.bfloat16),
            pltpu.VMEM((stas, ntemp // 2, 3 * TLEN), jnp.bfloat16),
            pltpu.VMEM((lines, WIN), jnp.float32),
            pltpu.VMEM((3 * stas, LANES, WIN), jnp.bfloat16),
            pltpu.VMEM((stas, WIN), jnp.float32),
            pltpu.VMEM((stas * (ntemp // 2), LANES), jnp.float32),
            pltpu.VMEM((stas * (ntemp // 2) * ROWS, LANES), jnp.float32),
            pltpu.VMEM((2 * OUTR * 8, LANES), jnp.float32),
            pltpu.VMEM((peers - 1, mine, BLOCK), jnp.int16),
            pltpu.VMEM((peers - 1, 16, LANES), jnp.bfloat16),
            pltpu.VMEM((peers - 1, mine, BLOCK), jnp.int16),
            pltpu.VMEM((peers - 1, 16, LANES), jnp.bfloat16),
            pltpu.SemaphoreType.DMA((3,)),
            pltpu.SemaphoreType.DMA((2,)),
            dma, dma, dma, dma,
        ],
        compiler_params=pltpu.CompilerParams(
            collective_id=0, has_side_effects=True, vmem_limit_bytes=63 * 1024 * 1024 + 512 * 1024
        ),
        name="stack",
    )(jnp.transpose(waveforms, (1, 0, 2)), templates, moveouts, gap_masks)


def solution(mesh):
    in_specs = (P("sta", None, "tm"), P("sta", None, None), P("sta", None), P("sta", None))
    out_specs = P("sta", "tm")
    return jax.shard_map(local, mesh=mesh, in_specs=in_specs, out_specs=out_specs, check_vma=False)
```

```python
import functools

import jax
import jax.numpy as jnp
from jax import lax
from jax.experimental import pallas as pl
from jax.experimental.pallas import tpu as pltpu
from jax.sharding import PartitionSpec as P

TLEN = 256
MAXMOVE = 1792
BLOCK = 2048
EPSILON = 1e-06
WIN = 2 * BLOCK
COLS = BLOCK + MAXMOVE
LANES = 128
ROWS = COLS // LANES + 1
OUTR = BLOCK // LANES
TILE = 1280
LEVELS = 32767.0
MESH = pl.DeviceIdType.MESH


def left(value, amount):
    size = value.shape[-1]
    return value if amount % size == 0 else pltpu.roll(value, (-amount) % size, axis=1)


def stack_kernel(
    peers, blocks, stas, x_ref, w_hbm, lag_hbm, gap_hbm, out_ref,
    w_ref, lag_ref, gap_ref, x_mine, nxt, wt_all, wave, hank, scale, tscale, corr, stack, q_send, m_send, q_recv, m_recv,
    load_sem, halo_sem, qs_sem, qr_sem, ms_sem, mr_sem,
):
    ntemp = w_ref.shape[2]
    mine = ntemp // peers
    groups = mine // 8
    me_sta = lax.axis_index("sta")
    me_tm = lax.axis_index("tm")
    before = lax.rem(me_tm + blocks - 1, blocks)
    after = lax.rem(me_tm + 1, blocks)
    half = peers // 2

    loads = [
        pltpu.make_async_copy(w_hbm, w_ref, load_sem.at[0]),
        pltpu.make_async_copy(lag_hbm, lag_ref, load_sem.at[1]),
        pltpu.make_async_copy(gap_hbm, gap_ref, load_sem.at[2]),
    ]
    for load in loads:
        load.start()
    barrier = pltpu.get_barrier_semaphore()
    for other in (before, after):
        pl.semaphore_signal(barrier, inc=1, device_id={"tm": other}, device_id_type=MESH)
    for d in range(1, peers):
        pl.semaphore_signal(barrier, inc=1, device_id={"sta": lax.rem(me_sta + d, peers)}, device_id_type=MESH)
    lines = x_mine.shape[0]
    records = [x_ref[c] for c in range(3)] + [jnp.zeros((lines - 3 * stas, BLOCK), jnp.bfloat16)]
    wave[:, :BLOCK] = jnp.concatenate([part.astype(jnp.float32) for part in records], axis=0)
    x_mine[...] = wave[:, :BLOCK].astype(jnp.bfloat16)
    pl.semaphore_wait(barrier, peers + 1)

    halo = pltpu.make_async_remote_copy(
        src_ref=x_mine, dst_ref=nxt, send_sem=halo_sem.at[0], recv_sem=halo_sem.at[1],
        device_id={"tm": before}, device_id_type=MESH,
    )
    halo.start()

    wide = ntemp // 2

    def prepare(side):
        first = pl.multiple_of(side * wide, wide)

        def template_scale(s, carry):
            w = w_ref[s, :, pl.ds(first, wide)]
            wf = w.astype(jnp.float32)
            te = jnp.sum(wf * wf, axis=0, keepdims=True) / (3 * TLEN)
            across = jnp.broadcast_to(lax.rsqrt(te + EPSILON), (LANES, wide))
            tscale[pl.ds(pl.multiple_of(s * wide, wide), wide), :] = jnp.transpose(across)
            wt_all[s] = jnp.transpose(w)
            return carry

        lax.fori_loop(0, stas, template_scale, 0)

    def build(start, size, keep):
        sub8 = lax.broadcasted_iota(jnp.int32, (8, size), 0)

        def line(i, carry):
            base = jnp.broadcast_to(wave[pl.ds(i, 1), start : start + size], (8, size))
            for bit in (1, 2, 4):
                base = jnp.where((sub8 & bit) != 0, left(base, bit), base)
            for a in range(8):
                pair = jnp.concatenate([left(base, 16 * a), left(base, 16 * a + 8)], axis=0)
                hank[i, 16 * a : 16 * (a + 1), start : start + keep] = pair[:, :keep].astype(jnp.bfloat16)
            return carry

        lax.fori_loop(0, 3 * stas, line, 0)

    build(0, BLOCK, BLOCK - LANES)
    for load in loads:
        load.wait()
    prepare(1 - me_sta // half)
    halo.wait()

    present = (me_tm < blocks - 1).astype(jnp.float32)
    wave[:, BLOCK:] = nxt[...].astype(jnp.float32) * present
    squares = wave[...] * wave[...]
    run = squares[:stas] + squares[stas : 2 * stas] + squares[2 * stas : 3 * stas]
    step = 1
    while step < TLEN:
        run = run + left(run, step)
        step *= 2
    row = lax.rsqrt(run / (3 * TLEN) + EPSILON) * (1.0 / (3 * TLEN))
    lane = lax.broadcasted_iota(jnp.int32, (stas, WIN), 1)
    sub = lax.broadcasted_iota(jnp.int32, (stas, WIN), 0)
    alive = jnp.zeros((stas, WIN), jnp.int32)
    later = lax.min(me_tm + 1, blocks - 1)
    for s in range(stas):
        alive = jnp.where(sub == s, jnp.where(lane < BLOCK, gap_ref[s, me_tm], gap_ref[s, later]), alive)
    scale[...] = row * alive.astype(jnp.float32)
    build(BLOCK - LANES, BLOCK + LANES, BLOCK + LANES)

    lanes = lax.broadcasted_iota(jnp.int32, (OUTR, LANES), 1)
    corr_rows = wide * ROWS

    def correlate():
        def station(s, carry):
            wt = wt_all[s]
            ts = tscale[pl.ds(pl.multiple_of(s * wide, wide), wide), :]

            def tile(i, carry):
                start = pl.multiple_of(i * TILE, TILE)
                parts = []
                for c in range(3):
                    parts.append(hank[c * stas + s, :, pl.ds(start, TILE)])
                    parts.append(hank[c * stas + s, :, pl.ds(start + LANES, TILE)])
                rhs = jnp.concatenate(parts, axis=0)
                prod = lax.dot_general(wt, rhs, (((1,), (0,)), ((), ())), preferred_element_type=jnp.float32)
                prod = prod * scale[pl.ds(s, 1), pl.ds(start, TILE)]
                for h in range(TILE // LANES):
                    part = prod[:, LANES * h : LANES * (h + 1)] * ts
                    for g in range(wide // 8):
                        at = s * corr_rows + g * 8 * ROWS + i * (TILE // LANES) + h
                        corr[pl.ds(at, 8, stride=ROWS), :] = part[8 * g : 8 * g + 8]
                return carry

            return lax.fori_loop(0, COLS // TILE, tile, carry)

        lax.fori_loop(0, stas, station, 0)

    def shift_group(dest, g, slot):
        for k in range(8):
            total = None
            for s in range(stas):
                lag = lag_ref[s, dest * mine + g * 8 + k]
                r = lag & (LANES - 1)
                at = s * corr_rows + (lax.rem(dest, half) * mine + g * 8 + k) * ROWS + (lag >> 7)
                lo = corr[pl.ds(at, OUTR), :]
                hi = corr[pl.ds(at + 1, OUTR), :]
                term = pltpu.roll(jnp.where(lanes >= r, lo, hi), (LANES - r) & (LANES - 1), axis=1)
                total = term if total is None else total + term
            stack[pl.ds(slot * 8 * OUTR + k, OUTR, stride=8), :] = total

    def rows_copy(i, gp, dest):
        rows = pl.ds(pl.multiple_of(gp * 16, 16), 16)
        return pltpu.make_async_remote_copy(
            src_ref=q_send.at[i, rows], dst_ref=q_recv.at[i, rows],
            send_sem=qs_sem.at[i, gp], recv_sem=qr_sem.at[i, gp],
            device_id={"sta": dest}, device_id_type=MESH,
        )

    def scale_copy(i, dest):
        return pltpu.make_async_remote_copy(
            src_ref=m_send.at[i], dst_ref=m_recv.at[i], send_sem=ms_sem.at[i], recv_sem=mr_sem.at[i],
            device_id={"sta": dest}, device_id_type=MESH,
        )

    def target(i):
        side = me_sta // half
        far = (1 - side) * half + lax.rem(me_sta + i, half)
        near = side * half + lax.rem(me_sta + 1 + i, half)
        return jnp.where(i < half, far, near)

    def chunk(i, carry):
        dest = target(i)

        lane16 = lax.broadcasted_iota(jnp.int32, (16, LANES), 1)

        def pair(gp, tops):
            for h in range(2):
                shift_group(dest, gp * 2 + h, h)
            rows = pl.ds(pl.multiple_of(gp * 16, 16), 16)
            big = None
            vals = []
            for p in range(OUTR):
                v = jnp.concatenate(
                    [stack[8 * p : 8 * p + 8, :], stack[8 * OUTR + 8 * p : 8 * OUTR + 8 * p + 8, :]], axis=0
                )
                vals.append(v)
                big = jnp.abs(v) if big is None else jnp.maximum(big, jnp.abs(v))
            top = jnp.max(big, axis=1, keepdims=True) * 1.01
            top16 = jnp.broadcast_to(jnp.maximum(top, 1e-30), (16, LANES)).astype(jnp.bfloat16)
            top32 = top16.astype(jnp.float32)
            inv = 1.0 / top32
            for p in range(OUTR):
                a = jnp.abs(vals[p]) * inv
                root = a * lax.rsqrt(jnp.maximum(a, 1e-30))
                level = (root * LEVELS + 0.5).astype(jnp.int32)
                level = jnp.where(vals[p] < 0.0, -level, level)
                q_send[i, rows, LANES * p : LANES * (p + 1)] = level.astype(jnp.int16)
            rows_copy(i, gp, dest).start()
            return jnp.where(lane16 == gp, top32, tops)

        tops = lax.fori_loop(0, groups // 2, pair, jnp.zeros((16, LANES), jnp.float32))
        m_send[i] = tops.astype(jnp.bfloat16)
        scale_copy(i, dest).start()
        return carry

    correlate()
    lax.fori_loop(0, half, chunk, 0)
    prepare(me_sta // half)
    correlate()
    lax.fori_loop(half, peers - 1, chunk, 0)

    def own(g, carry):
        shift_group(me_sta, g, 0)
        for p in range(OUTR):
            out_ref[pl.ds(pl.multiple_of(g * 8, 8), 8), LANES * p : LANES * (p + 1)] = stack[8 * p : 8 * p + 8, :]
        return carry

    lax.fori_loop(0, groups, own, 0)

    def collect(i, carry):
        scale_copy(i, target(i)).wait()

        def add(gp, carry):
            rows_copy(i, gp, target(i)).wait()
            rows = pl.ds(pl.multiple_of(gp * 16, 16), 16)
            lane16 = lax.broadcasted_iota(jnp.int32, (16, LANES), 1)
            tops = jnp.where(lane16 == gp, m_recv[i].astype(jnp.float32), 0.0)
            unit = jnp.sum(tops, axis=1, keepdims=True) * (1.0 / (LEVELS * LEVELS))
            for p in range(OUTR):
                level = q_recv[i, rows, LANES * p : LANES * (p + 1)].astype(jnp.int32).astype(jnp.float32)
                out_ref[rows, LANES * p : LANES * (p + 1)] += level * jnp.abs(level) * unit
            return carry

        return lax.fori_loop(0, mine // 16, add, carry)

    lax.fori_loop(0, peers - 1, collect, 0)


def local(waveforms, templates, moveouts, gap_masks):
    stas = waveforms.shape[0]
    ntemp = templates.shape[2]
    peers, blocks = lax.axis_size("sta"), lax.axis_size("tm")
    mine = ntemp // peers
    lines = -(-3 * stas // 16) * 16
    vmem = pl.BlockSpec(memory_space=pltpu.VMEM)
    hbm = pl.BlockSpec(memory_space=pltpu.HBM)
    dma = pltpu.SemaphoreType.DMA((peers - 1,))
    many = pltpu.SemaphoreType.DMA((peers - 1, mine // 16))
    return pl.pallas_call(
        functools.partial(stack_kernel, peers, blocks, stas),
        out_shape=jax.ShapeDtypeStruct((mine, BLOCK), jnp.float32),
        in_specs=[vmem, hbm, hbm, hbm],
        out_specs=vmem,
        scratch_shapes=[
            pltpu.VMEM(templates.shape, jnp.bfloat16),
            pltpu.SMEM(moveouts.shape, jnp.int32),
            pltpu.SMEM(gap_masks.shape, jnp.int32),
            pltpu.VMEM((lines, BLOCK), jnp.bfloat16),
            pltpu.VMEM((lines, BLOCK), jnp.bfloat16),
            pltpu.VMEM((stas, ntemp // 2, 3 * TLEN), jnp.bfloat16),
            pltpu.VMEM((lines, WIN), jnp.float32),
            pltpu.VMEM((3 * stas, LANES, WIN), jnp.bfloat16),
            pltpu.VMEM((stas, WIN), jnp.float32),
            pltpu.VMEM((stas * (ntemp // 2), LANES), jnp.float32),
            pltpu.VMEM((stas * (ntemp // 2) * ROWS, LANES), jnp.float32),
            pltpu.VMEM((2 * OUTR * 8, LANES), jnp.float32),
            pltpu.VMEM((peers - 1, mine, BLOCK), jnp.int16),
            pltpu.VMEM((peers - 1, 16, LANES), jnp.bfloat16),
            pltpu.VMEM((peers - 1, mine, BLOCK), jnp.int16),
            pltpu.VMEM((peers - 1, 16, LANES), jnp.bfloat16),
            pltpu.SemaphoreType.DMA((3,)),
            pltpu.SemaphoreType.DMA((2,)),
            many, many, dma, dma,
        ],
        compiler_params=pltpu.CompilerParams(
            collective_id=0, has_side_effects=True, vmem_limit_bytes=63 * 1024 * 1024 + 512 * 1024
        ),
        name="stack",
    )(jnp.transpose(waveforms, (1, 0, 2)), templates, moveouts, gap_masks)


def solution(mesh):
    in_specs = (P("sta", None, "tm"), P("sta", None, None), P("sta", None), P("sta", None))
    out_specs = P("sta", "tm")
    return jax.shard_map(local, mesh=mesh, in_specs=in_specs, out_specs=out_specs, check_vma=False)
```
